32 devices in a mesh: grp: 4 (over y, x), dev: 8 (over z, core).
Axes of the slice: x: 2, y: 2, z: 4, core: 2. Of those that a mesh axis runs over, the one named last changes fastest.
Arguments:
- features: bfloat16 [2048, 32, 512], P(('grp', 'dev')), may hold values from -6 to 6
- occupancy: int32 [2048, 512], P(('grp', 'dev')), may hold values 0 or 1
- neighbours: int32 [2048, 27], P(('grp', 'dev')), may hold values from -1 to 2047, as said below
- conv_weight: bfloat16 [32, 32, 3, 3, 3], replicated, may hold values from -0.21875 to 0.21875
- conv_bias: float32 [32], replicated, may hold values from -3 to 3
- point_brick: int32 [262144], P(('grp', 'dev')), may hold values from 0 to 2047, as said below
- point_cell: int32 [262144], P(('grp', 'dev')), may hold values from 0 to 438, as said below
- point_frac: float32 [3, 262144], P(None, ('grp', 'dev')), may hold values from 0 to 1
- decoder_in: bfloat16 [64, 32], replicated, may hold values from -1 to 1
- decoder_bias: float32 [64], replicated, may hold values from -3 to 3
- decoder_out: bfloat16 [64], replicated, may hold values from -0.75 to 0.75
Outputs:
- block_out: bfloat16 [2048, 32, 512], P(('grp', 'dev'))
- point_value: float32 [262144], P(('grp', 'dev'))
The draws below stay inside these ranges and needn't reach their ends.
Inputs may be any that keep to these rules, and one draw needn't show every extreme that they name: `neighbours`: entry 9 (dx + 1) + 3 (dy + 1) + (dz + 1) of a brick's list names the brick displaced by (dx, dy, dz) bricks, or -1 if there is none. Bricks are numbered device by device in the order of grp then dev, 64 to a device. A brick named at dx = -1 lies on the previous device, at dx = 0 on the brick's own device, at dx = +1 on the next device. The relation is symmetric and entry 13 is the brick itself. `point_brick`: the point rows of one device name bricks of any one device at most 512 times, and some device's bricks are named exactly 512 times by the rows of every device. `point_cell`: 64 x + 8 y + z of the lower corner (x, y, z) of the cell that holds the point, each of x, y, z from 0 to 6.
All inputs are finite; a program needn't handle non-finite values. No bound on the sum of `occupancy` on one device may be relied on, other than what follows from the above.
Results may differ from the reference program's by a relative error of at most 0.0044.
Values may be sent and summed in bfloat16 or wider, within the bound.
A program may use at most 128 MiB of HBM per device.

```python
import jax
import jax.numpy as jnp
import numpy as np
from jax import lax

C = 32
HID = 64
VOX = 512
BRICK_DEV = 64
P_DEV = 8192
BRICKS = 2048
POINTS = 262144


def draw_neighbours(key, part):
    columns = BRICK_DEV // 2
    planes = BRICKS // BRICK_DEV
    heights = jax.random.randint(key, (planes, columns), 0, 3)
    brick_ids = jnp.arange(BRICKS, dtype=jnp.int32)
    plane = brick_ids // BRICK_DEV
    column = brick_ids % BRICK_DEV // 2
    layer = brick_ids % 2
    height = heights[plane, column] + layer
    listed = []
    for step_x in (-1, 0, 1):
        for step_y in (-1, 0, 1):
            for step_z in (-1, 0, 1):
                other_plane = plane + step_x
                other_column = column + step_y
                inside = (other_plane >= 0) & (other_plane < planes) & (other_column >= 0) & (other_column < columns)
                plane_safe = jnp.clip(other_plane, 0, planes - 1)
                column_safe = jnp.clip(other_column, 0, columns - 1)
                other_layer = height + step_z - heights[plane_safe, column_safe]
                exists = inside & (other_layer >= 0) & (other_layer <= 1)
                listed.append(jnp.where(exists, plane_safe * BRICK_DEV + column_safe * 2 + other_layer, -1))
    return jnp.stack(listed, axis=1).astype(jnp.int32)


def draw_point_brick(key, part):
    device_total = BRICKS // BRICK_DEV
    capacity = 2 * P_DEV // device_total
    key_hot, key_order, key_weight, key_local, key_shuffle = jax.random.split(key, 5)
    hottest = jax.random.randint(key_hot, (), 0, device_total)
    device_ids = jnp.arange(device_total, dtype=jnp.int32)
    scores = jax.random.randint(key_order, (device_total, device_total), 0, 1 << 20) * device_total + device_ids[None, :]
    scores = jnp.where(device_ids[None, :] == hottest, -1, scores)
    ranking = jnp.argsort(scores, axis=1).astype(jnp.int32)
    weights = jax.random.randint(key_weight, (device_total, device_total), capacity // 2, capacity + 1)
    weights = weights.at[:, 0].set(capacity)
    earlier = jnp.cumsum(weights, axis=1) - weights
    counts = jnp.clip(P_DEV - earlier, 0, weights)
    ends = jnp.cumsum(counts, axis=1)
    row_ids = jnp.arange(P_DEV, dtype=jnp.int32)
    position = jax.vmap(lambda edges: jnp.searchsorted(edges, row_ids, side='right'))(ends).astype(jnp.int32)
    target = jnp.take_along_axis(ranking, position, axis=1)
    shuffle_scores = jax.random.randint(key_shuffle, (device_total, P_DEV), 0, 1 << 12) * P_DEV + row_ids[None, :]
    shuffle = jnp.argsort(shuffle_scores, axis=1).astype(jnp.int32)
    target = jnp.take_along_axis(target, shuffle, axis=1)
    local_brick = jax.random.randint(key_local, (device_total, P_DEV), 0, BRICK_DEV)
    return (target * BRICK_DEV + local_brick).reshape(-1).astype(jnp.int32)


def draw_point_cell(key, part):
    corner = jax.random.randint(key, (3, POINTS), 0, 7)
    return (corner[0] * 64 + corner[1] * 8 + corner[2]).astype(jnp.int32)


def with_ends(result, rng, low, top_value):
    shape = result.shape
    spot = [jax.random.randint(jax.random.fold_in(rng, axis), (), 0, shape[axis]) for axis in range(len(shape))]
    result = result.at[tuple(spot)].set(low)
    longest = shape.index(max(shape))
    spot[longest] = (spot[longest] + 1) % shape[longest]
    return result.at[tuple(spot)].set(top_value)


def steps_of(key, shape, shards, least, high):
    gain, own = 1.0, jax.random.fold_in(key, 6)
    for dim, blocks in shards:
        steps = jnp.exp(jax.random.uniform(jax.random.fold_in(own, dim), (blocks,), jnp.float32, least / len(shards), high / len(shards)))
        gain = gain * jnp.repeat(steps, shape[dim] // blocks).reshape([-1 if axis == dim else 1 for axis in range(len(shape))])
    return gain


def normal_values(stream_key, extent, scale, limit, cuts=(), held_as=jnp.bfloat16):
    values = scale * jax.random.normal(stream_key, extent, jnp.float32)
    if cuts:
        values = values * steps_of(stream_key, extent, cuts, -0.22, 0.18)
    return jnp.clip(values, -limit, limit).astype(held_as)


def setup_inputs(seed: int = 0) -> dict:
    keys = jax.random.split(jax.random.key(seed), 12)
    features = normal_values(keys[0], (BRICKS, C, VOX), 1.0, 6.0, ((0, 32),))
    occupancy = with_ends((jax.random.randint(keys[1], (BRICKS, VOX), 0, 2) < 1).astype(jnp.int32), jax.random.fold_in(keys[1], 1), 0, 1)
    neighbours = draw_neighbours(jax.random.fold_in(keys[11], 71), 0)
    conv_weight = normal_values(keys[3], (C, C, 3, 3, 3), (27 * C) ** -0.5, 0.21875)
    conv_bias = normal_values(keys[4], (C,), 0.5, 3.0, (), jnp.float32)
    point_brick = draw_point_brick(jax.random.fold_in(keys[11], 71), 0)
    point_cell = draw_point_cell(jax.random.fold_in(keys[11], 71), 0)
    point_frac = jnp.clip(1.0 * jax.random.uniform(keys[7], (3, POINTS), jnp.float32) ** steps_of(keys[7], (3, POINTS), ((1, 32),), -0.2, 0.2), 0.0, 1.0)
    decoder_in = normal_values(keys[8], (HID, C), C ** -0.5, 1.0)
    decoder_bias = normal_values(keys[9], (HID,), 0.5, 3.0, (), jnp.float32)
    decoder_out = normal_values(keys[10], (HID,), HID ** -0.5, 0.75)
    return dict(features=features, occupancy=occupancy, neighbours=neighbours, conv_weight=conv_weight, conv_bias=conv_bias, point_brick=point_brick, point_cell=point_cell, point_frac=point_frac, decoder_in=decoder_in, decoder_bias=decoder_bias, decoder_out=decoder_out)


def axis_span(direction):
    if direction < 0:
        return [7], [0]
    if direction > 0:
        return [0], [9]
    return list(range(8)), list(range(1, 9))


def tile_tables():
    voxel_lists = []
    placement_all = []
    for step_x in (-1, 0, 1):
        for step_y in (-1, 0, 1):
            for step_z in (-1, 0, 1):
                source_x, target_x = axis_span(step_x)
                source_y, target_y = axis_span(step_y)
                source_z, target_z = axis_span(step_z)
                voxel_lists.append(np.array([i * 64 + j * 8 + k for i in source_x for j in source_y for k in source_z], np.int32))
                placement_all.extend([i * 100 + j * 10 + k for i in target_x for j in target_y for k in target_z])
    return voxel_lists, np.argsort(np.array(placement_all)).astype(np.int32)


def trilinear(flat_table, base_column, fraction):
    summed = jnp.zeros((flat_table.shape[0], base_column.shape[0]), jnp.float32)
    for corner in range(8):
        corner_bits = [(corner >> 2) & 1, (corner >> 1) & 1, corner & 1]
        weight = jnp.ones_like(fraction[0])
        for axis_id in range(3):
            weight = weight * (fraction[axis_id] if corner_bits[axis_id] else 1.0 - fraction[axis_id])
        column = base_column + corner_bits[0] * 64 + corner_bits[1] * 8 + corner_bits[2]
        summed = summed + weight[None, :] * jnp.take(flat_table, column, axis=1).astype(jnp.float32)
    return summed


def decoder(sample, decoder_in, decoder_bias, decoder_out):
    hidden = jax.nn.relu(jnp.dot(decoder_in, sample.astype(jnp.bfloat16), preferred_element_type=jnp.float32) + decoder_bias[:, None]).astype(jnp.bfloat16)
    return jnp.dot(decoder_out[None, :], hidden, preferred_element_type=jnp.float32)[0]


def reference(features, occupancy, neighbours, conv_weight, conv_bias, point_brick, point_cell, point_frac, decoder_in, decoder_bias, decoder_out):
    voxel_lists, tile_order = tile_tables()
    masked = features * occupancy[:, None, :].astype(features.dtype)
    kernel = conv_weight.astype(jnp.float32)

    def one_block(block_args):
        listed_all, own_masked, own_occupancy = block_args
        pieces = []
        for neighbour_slot in range(27):
            listed = listed_all[:, neighbour_slot]
            present = listed >= 0
            rows_taken = jnp.take(masked, jnp.where(present, listed, 0).astype(jnp.int32), axis=0)[:, :, voxel_lists[neighbour_slot]]
            pieces.append(rows_taken * present[:, None, None].astype(rows_taken.dtype))
        padded = jnp.concatenate(pieces, axis=2)[:, :, tile_order].reshape(BRICK_DEV, C, 10, 10, 10).astype(jnp.float32)
        convolved = lax.conv_general_dilated(padded, kernel, (1, 1, 1), "VALID", dimension_numbers=("NCDHW", "OIDHW", "NCDHW"), precision=lax.Precision.HIGHEST).reshape(BRICK_DEV, C, VOX)
        occupied = own_occupancy[:, None, :].astype(jnp.float32)
        return (own_masked.astype(jnp.float32) + occupied * jax.nn.relu(convolved + conv_bias[None, :, None])).astype(jnp.bfloat16)

    block_out = lax.map(one_block, (neighbours.reshape(-1, BRICK_DEV, 27), masked.reshape(-1, BRICK_DEV, C, VOX), occupancy.reshape(-1, BRICK_DEV, VOX))).reshape(BRICKS, C, VOX)
    flat_table = jnp.transpose(block_out, (1, 0, 2)).reshape(C, BRICKS * VOX)
    sample = trilinear(flat_table, (point_brick * VOX + point_cell).astype(jnp.int32), point_frac)
    point_value = decoder(sample, decoder_in, decoder_bias, decoder_out)
    return block_out, point_value
```

```python
import functools

import jax
import jax.numpy as jnp
from jax import lax
from jax.experimental import pallas as pl
from jax.experimental.pallas import tpu as pltpu
from jax.sharding import PartitionSpec as P

F32 = jnp.float32
BF16 = jnp.bfloat16
VMEM_BYTES = 56 * 1024 * 1024


def from_behind(value, axis, steps):
    count = lax.axis_size(axis)
    initial, last = (max(0, -steps), min(count, count - steps))
    return lax.ppermute(value, axis, [(source, source + steps) for source in range(initial, last)])


def iota(shape, axis):
    return lax.broadcasted_iota(jnp.int32, shape, axis)


def shifted(own, below, above, step, stride, coord):
    lanes = own.shape[1]
    if step == 0:
        return own
    if step > 0:
        return jnp.where(
            coord < 7, pltpu.roll(own, lanes - stride, 1), pltpu.roll(above, 7 * stride, 1)
        )
    return jnp.where(
        coord > 0, pltpu.roll(own, stride, 1), pltpu.roll(below, lanes - 7 * stride, 1)
    )


def conv_kernel(per_step, nb_ref, own_ref, prev_ref, next_ref, occ_ref, w_ref, bias_ref, out_ref, x_ref):
    lane = iota((32, 128), 1)
    z = lane & 7
    y = (lane >> 3) & 7
    low_half = lane < 64
    step_id = pl.program_id(0)
    together = x_ref.shape[0]

    def one_brick(i, k):
        b = step_id * per_step + i
        for col in range(5):
            pieces = []
            for slot in range(9):
                if col < 4:
                    piece = own_ref[nb_ref[b * 27 + 9 + slot], :, col * 128 : (col + 1) * 128]
                else:
                    piece = jnp.where(
                        low_half,
                        next_ref[nb_ref[b * 27 + 18 + slot]],
                        prev_ref[nb_ref[b * 27 + slot]],
                    )
                pieces.append(piece)
            for tz in (-1, 0, 1):
                rows = [
                    shifted(pieces[3 * j + 1], pieces[3 * j], pieces[3 * j + 2], tz, 1, z)
                    for j in range(3)
                ]
                for ty in (-1, 0, 1):
                    moved = shifted(rows[1], rows[0], rows[2], ty, 8, y)
                    at = ((ty + 1) * 3 + tz + 1) * 32
                    x_ref[k, at : at + 32, col * 128 : (col + 1) * 128] = moved
        conv = jnp.dot(w_ref[...], x_ref[k], preferred_element_type=F32)
        behind = [
            pltpu.roll(conv[0:32, c * 128 : (c + 1) * 128], 64, 1) for c in (4, 0, 1, 2, 3)
        ]
        ahead = [
            pltpu.roll(conv[64:96, c * 128 : (c + 1) * 128], 64, 1) for c in (0, 1, 2, 3, 4)
        ]
        for col in range(4):
            lanes = slice(col * 128, (col + 1) * 128)
            total = conv[32:64, lanes]
            total = total + jnp.where(low_half, behind[col], behind[col + 1])
            total = total + jnp.where(low_half, ahead[col], ahead[col + 1])
            occupied = occ_ref[b, :, lanes].astype(F32)
            center = own_ref[b, :, lanes].astype(F32)
            out_ref[i, :, lanes] = (
                center + occupied * jnp.maximum(total + bias_ref[...], 0.0)
            ).astype(BF16)

    def some_bricks(j, carry):
        for k in range(together):
            one_brick(j * together + k, k)
        return carry

    lax.fori_loop(0, per_step // together, some_bricks, 0)


def conv_block(masked, previous, following, local_nb, occupancy, conv_weight, conv_bias):
    bricks = masked.shape[0] - 1
    weight = jnp.transpose(conv_weight, (2, 0, 3, 4, 1)).reshape(96, 288)
    per_step = 8

    def whole(*shape):
        return pl.BlockSpec(shape, lambda i, nb: (0,) * len(shape))

    return pl.pallas_call(
        functools.partial(conv_kernel, per_step),
        grid_spec=pltpu.PrefetchScalarGridSpec(
            num_scalar_prefetch=1,
            grid=(bricks // per_step,),
            in_specs=[
                whole(bricks + 1, 32, 512),
                whole(bricks + 1, 32, 128),
                whole(bricks + 1, 32, 128),
                whole(bricks, 1, 512),
                whole(96, 288),
                whole(32, 1),
            ],
            out_specs=pl.BlockSpec((per_step, 32, 512), lambda i, nb: (i, 0, 0)),
            scratch_shapes=[pltpu.VMEM((4, 288, 640), BF16)],
        ),
        out_shape=jax.ShapeDtypeStruct((bricks, 32, 512), BF16),
        compiler_params=pltpu.CompilerParams(vmem_limit_bytes=VMEM_BYTES),
        cost_estimate=pl.CostEstimate(flops=4 * 10**9, bytes_accessed=6 * 2**20, transcendentals=0),
        name="conv_block",
    )(local_nb, masked, previous, following, occupancy[:, None, :], weight, conv_bias[:, None])


def dispatch_kernel(shift, width, brick_ref, cell_ref, frac_ref, send_ref, slot_ref, acc_ref):
    devices, _, capacity = send_ref.shape
    points = brick_ref.shape[1]
    before = (iota((width, width), 0) < iota((width, width), 1)).astype(BF16)
    acc_ref[...] = jnp.zeros_like(acc_ref)

    def block(i, offset):
        at = pl.ds(pl.multiple_of(i * width, width), width)
        brick = brick_ref[:, at]
        owner = lax.shift_right_logical(brick, shift)
        hit = iota((devices, width), 0) == owner
        hits = hit.astype(F32)
        rank = jnp.dot(hits.astype(BF16), before, preferred_element_type=F32) + offset
        slot = jnp.sum(hits * rank, axis=0, keepdims=True).astype(jnp.int32)
        slot_ref[:, at] = slot
        index = (brick - lax.shift_left(owner, shift)) * 512 + cell_ref[:, at]
        words = [index] + [
            (frac_ref[a : a + 1, at] * 65535.0 + 0.5).astype(jnp.int32) for a in range(3)
        ]
        rows = []
        for word in words:
            rows.append((hits * lax.shift_right_logical(word, 8).astype(F32)).astype(BF16))
            rows.append((hits * (word & 255).astype(F32)).astype(BF16))
        spread = (iota((capacity, width), 0) == slot).astype(F32).astype(BF16)
        acc_ref[...] += lax.dot_general(
            jnp.concatenate(rows, axis=0),
            spread,
            (((1,), (1,)), ((), ())),
            preferred_element_type=F32,
        )
        return offset + jnp.sum(hits, axis=1, keepdims=True)

    lax.fori_loop(0, points // width, block, jnp.zeros((devices, 1), F32))
    for word in range(4):
        high = acc_ref[2 * word * devices : (2 * word + 1) * devices, :]
        low = acc_ref[(2 * word + 1) * devices : (2 * word + 2) * devices, :]
        send_ref[:, word, :] = high * 256.0 + low


def dispatch(point_brick, point_cell, point_frac, devices, capacity, bricks):
    points = point_brick.shape[0]
    shift = bricks.bit_length() - 1
    assert bricks == 1 << shift
    return pl.pallas_call(
        functools.partial(dispatch_kernel, shift, 512),
        out_shape=(
            jax.ShapeDtypeStruct((devices, 4, capacity), F32),
            jax.ShapeDtypeStruct((1, points), jnp.int32),
        ),
        scratch_shapes=[pltpu.VMEM((8 * devices, capacity), F32)],
        compiler_params=pltpu.CompilerParams(vmem_limit_bytes=VMEM_BYTES),
        name="dispatch",
    )(point_brick[None, :], point_cell[None, :], point_frac)


def sample_kernel(blocks_ref, recv_ref, din_ref, bias_ref, dout_ref, out_ref, table_ref):
    sources, _, capacity = recv_ref.shape
    depth = table_ref.shape[1]
    bricks = depth // 8

    def turn(c, carry):
        for j in range(4):
            part = blocks_ref[c, :, j * 128 : (j + 1) * 128].astype(F32)
            both = jnp.concatenate([part, pltpu.roll(part, 64, 1)], axis=0)
            table_ref[pl.ds(pl.multiple_of(c * 64, 64), 64), j * 2 * bricks : (j + 1) * 2 * bricks] = (
                both.T[:64].astype(BF16)
            )
        return carry

    lax.fori_loop(0, 32, turn, 0)

    def chunk(s, carry):
        index = recv_ref[s, 0:1, :].astype(jnp.int32)
        fx, fy, fz = (recv_ref[s, a : a + 1, :] * (1.0 / 65535.0) for a in (1, 2, 3))
        x0 = lax.shift_right_logical(index, 6) & 7
        xb = x0 * bricks + lax.shift_right_logical(index, 9)
        row = iota((depth, capacity), 0)
        along_x = jnp.where(
            row == xb, 1.0 - fx, jnp.where(row == xb + bricks, fx, 0.0)
        ).astype(BF16)
        yz = iota((64, capacity), 0)
        y0 = lax.shift_right_logical(index, 3) & 7
        z0 = index & 7
        ry, rz = lax.shift_right_logical(yz, 3), yz & 7
        along_y = jnp.where(ry == y0, 1.0 - fy, jnp.where(ry == y0 + 1, fy, 0.0))
        along_z = jnp.where(rz == z0, 1.0 - fz, jnp.where(rz == z0 + 1, fz, 0.0))
        weight = along_y * along_z
        sums = []
        for part in range(4):
            found = jnp.dot(
                table_ref[part * 512 : (part + 1) * 512, :], along_x, preferred_element_type=F32
            )
            for c in range(8):
                rows = [
                    found[c * 64 + k : c * 64 + k + 8, :] * weight[k : k + 8, :]
                    for k in range(0, 64, 8)
                ]
                while len(rows) > 1:
                    rows = [p + q for p, q in zip(rows[::2], rows[1::2])]
                sums.append(rows[0])
        sample = jnp.concatenate(sums, axis=0).astype(BF16)
        hidden = jnp.maximum(
            jnp.dot(din_ref[...], sample, preferred_element_type=F32) + bias_ref[...],
            0.0,
        ).astype(BF16)
        out_ref[s] = jnp.sum(hidden.astype(F32) * dout_ref[...], axis=0, keepdims=True)
        return carry

    lax.fori_loop(0, sources, chunk, 0)


def sample_points(block_out, received, decoder_in, decoder_bias, decoder_out):
    bricks = block_out.shape[0]
    sources, _, capacity = received.shape
    return pl.pallas_call(
        sample_kernel,
        out_shape=jax.ShapeDtypeStruct((sources, 1, capacity), F32),
        scratch_shapes=[pltpu.VMEM((2048, bricks * 8), BF16)],
        compiler_params=pltpu.CompilerParams(vmem_limit_bytes=VMEM_BYTES),
        name="sample_points",
    )(
        jnp.transpose(block_out, (1, 0, 2)),
        received,
        jnp.repeat(decoder_in, 8, axis=1),
        decoder_bias[:, None],
        decoder_out.astype(F32)[:, None],
    )[:, 0, :]


def collect_kernel(shift, width, brick_ref, slot_ref, back_ref, out_ref):
    devices, capacity = back_ref.shape
    points = brick_ref.shape[1]
    back = back_ref[...]
    high = back.astype(BF16)
    rest = back - high.astype(F32)
    mid = rest.astype(BF16)
    low = (rest - mid.astype(F32)).astype(BF16)
    pieces = jnp.concatenate([high, mid, low], axis=0)

    def block(i, carry):
        at = pl.ds(pl.multiple_of(i * width, width), width)
        owner = lax.shift_right_logical(brick_ref[:, at], shift)
        spread = (iota((capacity, width), 0) == slot_ref[:, at]).astype(F32).astype(BF16)
        found = jnp.dot(pieces, spread, preferred_element_type=F32)
        value = found[:devices] + found[devices : 2 * devices] + found[2 * devices :]
        hit = iota((devices, width), 0) == owner
        out_ref[:, at] = jnp.sum(jnp.where(hit, value, 0.0), axis=0, keepdims=True)
        return carry

    lax.fori_loop(0, points // width, block, 0)


def collect(point_brick, slot, back, bricks):
    points = point_brick.shape[0]
    return pl.pallas_call(
        functools.partial(collect_kernel, bricks.bit_length() - 1, 512),
        out_shape=jax.ShapeDtypeStruct((1, points), F32),
        compiler_params=pltpu.CompilerParams(vmem_limit_bytes=VMEM_BYTES),
        name="collect",
    )(point_brick[None, :], slot, back)[0]


def per_device(
    features,
    occupancy,
    neighbours,
    conv_weight,
    conv_bias,
    point_brick,
    point_cell,
    point_frac,
    decoder_in,
    decoder_bias,
    decoder_out,
):
    axes = ("grp", "dev")
    bricks = features.shape[0]
    devices = lax.axis_size(axes)
    me = lax.axis_index(axes)
    capacity = 2 * point_brick.shape[0] // devices
    send, slot = dispatch(point_brick, point_cell, point_frac, devices, capacity, bricks)
    received = lax.all_to_all(send, axes, split_axis=0, concat_axis=0, tiled=True)
    masked = features * occupancy[:, None, :].astype(features.dtype)
    masked = jnp.pad(masked, ((0, 1), (0, 0), (0, 0)))
    previous = from_behind(masked[:, :, 384:], axes, 1)
    following = from_behind(masked[:, :, :128], axes, -1)
    first = (me + jnp.repeat(jnp.arange(-1, 2, dtype=jnp.int32), 9)) * bricks
    local_nb = jnp.where(
        neighbours >= 0, jnp.clip(neighbours - first[None, :], 0, bricks - 1), bricks
    ).reshape(-1)
    block_out = conv_block(
        masked, previous, following, local_nb, occupancy, conv_weight, conv_bias
    )
    values = sample_points(block_out, received, decoder_in, decoder_bias, decoder_out)
    back = lax.all_to_all(values, axes, split_axis=0, concat_axis=0, tiled=True)
    return block_out, collect(point_brick, slot, back, bricks)


def solution(mesh):
    axes = ("grp", "dev")
    return jax.shard_map(
        per_device,
        mesh=mesh,
        in_specs=(
            P(axes, None, None),
            P(axes, None),
            P(axes, None),
            P(),
            P(),
            P(axes),
            P(axes),
            P(None, axes),
            P(),
            P(),
            P(),
        ),
        out_specs=(P(axes, None, None), P(axes)),
        check_vma=False,
    )
```

```python
import functools

import jax
import jax.numpy as jnp
from jax import lax
from jax.experimental import pallas as pl
from jax.experimental.pallas import tpu as pltpu
from jax.sharding import PartitionSpec as P

F32 = jnp.float32
BF16 = jnp.bfloat16
VMEM_BYTES = 56 * 1024 * 1024


def from_behind(value, axis, steps):
    count = lax.axis_size(axis)
    initial, last = (max(0, -steps), min(count, count - steps))
    return lax.ppermute(value, axis, [(source, source + steps) for source in range(initial, last)])


def iota(shape, axis):
    return lax.broadcasted_iota(jnp.int32, shape, axis)


def conv_kernel(per_step, nb_ref, own_ref, prev_ref, next_ref, occ_ref, w_ref, bias_ref, out_ref, x_ref, edge_ref, prev_edge_ref, next_edge_ref):
    lane = iota((8, 128), 1)
    row = iota((8, 128), 0)
    bricks = own_ref.shape[0]

    def edges(lanes):
        both = jnp.where(
            iota(lanes.shape[:-1] + (128,), len(lanes.shape) - 1) < 32,
            pltpu.roll(lanes[..., 128:], 32, len(lanes.shape) - 1),
            pltpu.roll(lanes[..., :128], 32, len(lanes.shape) - 1),
        )
        again = pltpu.roll(both, 64, len(lanes.shape) - 1)
        return jnp.where(iota(both.shape, len(lanes.shape) - 1) < 64, both, again)

    @pl.when(pl.program_id(0) == 0)
    def _():
        def fill(b, carry):
            for x in range(8):
                edge_ref[b, x] = edges(own_ref[b, x])
            prev_edge_ref[b] = edges(prev_ref[b])
            next_edge_ref[b] = edges(next_ref[b])
            return carry

        lax.fori_loop(0, bricks, fill, 0)

    def moved(below, here, above):
        back = pltpu.roll(jnp.where(row == 7, below, here), 1, 0)
        forth = pltpu.roll(jnp.where(row == 0, above, here), 7, 0)
        return back, here, forth

    first = pl.program_id(0) * per_step

    def one_brick(i, carry):
        base = (first + i) * 27
        columns = []
        for x in range(-1, 9):
            group = 0 if x < 0 else (2 if x > 7 else 1)
            names = [nb_ref[base + group * 9 + slot] for slot in range(9)]
            if group == 0:
                whole, edge = (lambda n: prev_ref[n]), (lambda n: prev_edge_ref[n])
            elif group == 2:
                whole, edge = (lambda n: next_ref[n]), (lambda n: next_edge_ref[n])
            else:
                whole, edge = (lambda n: own_ref[n, x]), (lambda n: edge_ref[n, x])
            lines = [whole(names[3 * j + 1]) for j in range(3)]
            low = moved(*[line[:, :128] for line in lines])
            high = moved(*[line[:, 128:] for line in lines])
            ends = moved(
                *[
                    jnp.where((lane & 63) < 32, edge(names[3 * j]), edge(names[3 * j + 2]))
                    for j in range(3)
                ]
            )
            columns.append(
                [low[0], high[0], low[1], high[1], low[2], high[2]]
                + [jnp.where(lane < 64, ends[0], ends[2]), ends[1]]
            )
        for pair in range(5):
            at = pl.ds(pl.multiple_of(i * 80 + pair * 16, 16), 16)
            for k in range(8):
                x_ref[at, k * 128 : (k + 1) * 128] = jnp.concatenate(
                    [columns[2 * pair][k], columns[2 * pair + 1][k]], axis=0
                ).astype(BF16)
        return carry

    lax.fori_loop(0, per_step, one_brick, 0)
    found = jnp.dot(x_ref[...], w_ref[...], preferred_element_type=F32)
    for i in range(per_step):
        total = bias_ref[...]
        for tx in range(3):
            at = i * 80 + tx * 8
            total = total + found[at : at + 64, tx * 256 : (tx + 1) * 256]
        center = own_ref[first + i].reshape(64, 256)
        occupied = occ_ref[i].reshape(64, 256).astype(F32)
        out_ref[i] = (center + occupied * jnp.maximum(total, 0.0)).reshape(8, 8, 256)


def banded_weight(conv_weight):
    taps = jnp.transpose(conv_weight, (3, 1, 2, 4, 0))[:, :, :, ::-1, :].reshape(3, 32, 3, 96)
    wide = jnp.pad(taps, ((0, 0), (0, 0), (0, 0), (256, 256)))
    rows = []
    for z in range(-1, 9):
        start = 256 - (z - 1) * 32
        rows.append(wide[:, :, :, start : start + 256].reshape(3, 32, 768))
    own = jnp.stack(rows[1:9], axis=1).reshape(768, 768)
    ends = jnp.concatenate([rows[0], rows[9]], axis=1)
    return jnp.concatenate([own, ends[0], ends[2], ends[1], jnp.zeros_like(ends[1])], axis=0)


def conv_block(masked, previous, following, local_nb, occupancy, conv_weight, conv_bias):
    bricks = masked.shape[0] - 1
    weight = banded_weight(conv_weight)
    per_step = 8

    def whole(*shape):
        return pl.BlockSpec(shape, lambda i, nb: (0,) * len(shape))

    def part(*shape):
        return pl.BlockSpec((per_step,) + shape, lambda i, nb: (i,) + (0,) * len(shape))

    occupied = jnp.repeat(occupancy.reshape(bricks, 64, 8).astype(BF16), 32, axis=2)
    return pl.pallas_call(
        functools.partial(conv_kernel, per_step),
        grid_spec=pltpu.PrefetchScalarGridSpec(
            num_scalar_prefetch=1,
            grid=(bricks // per_step,),
            in_specs=[
                whole(bricks + 1, 8, 8, 256),
                whole(bricks + 1, 8, 256),
                whole(bricks + 1, 8, 256),
                part(64, 256),
                whole(1024, 768),
                whole(1, 256),
            ],
            out_specs=part(8, 8, 256),
            scratch_shapes=[
                pltpu.VMEM((per_step * 80, 1024), BF16),
                pltpu.VMEM((bricks + 1, 8, 8, 128), F32),
                pltpu.VMEM((bricks + 1, 8, 128), F32),
                pltpu.VMEM((bricks + 1, 8, 128), F32),
            ],
        ),
        out_shape=jax.ShapeDtypeStruct((bricks, 8, 8, 256), F32),
        compiler_params=pltpu.CompilerParams(vmem_limit_bytes=VMEM_BYTES),
        cost_estimate=pl.CostEstimate(flops=8 * 10**9, bytes_accessed=12 * 2**20, transcendentals=0),
        name="conv_block",
    )(local_nb, masked, previous, following, occupied, weight, jnp.tile(conv_bias, 8)[None, :])


def dispatch_kernel(shift, width, brick_ref, cell_ref, frac_ref, send_ref, slot_ref, acc_ref):
    devices, _, capacity = send_ref.shape
    points = brick_ref.shape[1]
    before = (iota((width, width), 0) < iota((width, width), 1)).astype(BF16)
    acc_ref[...] = jnp.zeros_like(acc_ref)

    def block(i, offset):
        at = pl.ds(pl.multiple_of(i * width, width), width)
        brick = brick_ref[:, at]
        owner = lax.shift_right_logical(brick, shift)
        hit = iota((devices, width), 0) == owner
        hits = hit.astype(F32)
        rank = jnp.dot(hits.astype(BF16), before, preferred_element_type=F32) + offset
        slot = jnp.sum(hits * rank, axis=0, keepdims=True).astype(jnp.int32)
        slot_ref[:, at] = slot
        index = (brick - lax.shift_left(owner, shift)) * 512 + cell_ref[:, at]
        words = [index] + [
            (frac_ref[a : a + 1, at] * 65535.0 + 0.5).astype(jnp.int32) for a in range(3)
        ]
        rows = []
        for word in words:
            rows.append((hits * lax.shift_right_logical(word, 8).astype(F32)).astype(BF16))
            rows.append((hits * (word & 255).astype(F32)).astype(BF16))
        spread = (iota((capacity, width), 0) == slot).astype(F32).astype(BF16)
        acc_ref[...] += lax.dot_general(
            jnp.concatenate(rows, axis=0),
            spread,
            (((1,), (1,)), ((), ())),
            preferred_element_type=F32,
        )
        return offset + jnp.sum(hits, axis=1, keepdims=True)

    lax.fori_loop(0, points // width, block, jnp.zeros((devices, 1), F32))
    for word in range(4):
        high = acc_ref[2 * word * devices : (2 * word + 1) * devices, :]
        low = acc_ref[(2 * word + 1) * devices : (2 * word + 2) * devices, :]
        send_ref[:, word, :] = high * 256.0 + low


def dispatch(point_brick, point_cell, point_frac, devices, capacity, bricks):
    points = point_brick.shape[0]
    shift = bricks.bit_length() - 1
    assert bricks == 1 << shift
    return pl.pallas_call(
        functools.partial(dispatch_kernel, shift, 512),
        out_shape=(
            jax.ShapeDtypeStruct((devices, 4, capacity), F32),
            jax.ShapeDtypeStruct((1, points), jnp.int32),
        ),
        scratch_shapes=[pltpu.VMEM((8 * devices, capacity), F32)],
        compiler_params=pltpu.CompilerParams(vmem_limit_bytes=VMEM_BYTES),
        name="dispatch",
    )(point_brick[None, :], point_cell[None, :], point_frac)


def sample_kernel(blocks_ref, recv_ref, din_ref, bias_ref, dout_ref, out_ref, table_ref):
    sources, _, capacity = recv_ref.shape
    depth = table_ref.shape[1]
    for x in range(8):
        table_ref[x * 256 : (x + 1) * 256, :] = blocks_ref[:, x].reshape(depth, 256).T.astype(BF16)

    def chunk(s, carry):
        index = recv_ref[s, 0:1, :].astype(jnp.int32)
        fx, fy, fz = (recv_ref[s, a : a + 1, :] * (1.0 / 65535.0) for a in (1, 2, 3))
        by = lax.shift_right_logical(index, 9) * 8 + (lax.shift_right_logical(index, 3) & 7)
        row = iota((depth, capacity), 0)
        along_y = jnp.where(
            row == by, 1.0 - fy, jnp.where(row == by + 1, fy, 0.0)
        ).astype(BF16)
        xz = iota((64, capacity), 0)
        x0 = lax.shift_right_logical(index, 6) & 7
        z0 = index & 7
        rx, rz = lax.shift_right_logical(xz, 3), xz & 7
        along_x = jnp.where(rx == x0, 1.0 - fx, jnp.where(rx == x0 + 1, fx, 0.0))
        along_z = jnp.where(rz == z0, 1.0 - fz, jnp.where(rz == z0 + 1, fz, 0.0))
        weight = along_x * along_z
        sample = jnp.zeros((32, capacity), F32)
        for part in range(4):
            found = jnp.dot(
                table_ref[part * 512 : (part + 1) * 512, :], along_y, preferred_element_type=F32
            )
            for j in range(16):
                k = part * 16 + j
                sample = sample + found[j * 32 : (j + 1) * 32, :] * weight[k : k + 1, :]
        sample = sample.astype(BF16)
        hidden = jnp.maximum(
            jnp.dot(din_ref[...], sample, preferred_element_type=F32) + bias_ref[...],
            0.0,
        ).astype(BF16)
        out_ref[s] = jnp.sum(hidden.astype(F32) * dout_ref[...], axis=0, keepdims=True)
        return carry

    lax.fori_loop(0, sources, chunk, 0)


def sample_points(blocks, received, decoder_in, decoder_bias, decoder_out):
    bricks = blocks.shape[0]
    sources, _, capacity = received.shape
    return pl.pallas_call(
        sample_kernel,
        out_shape=jax.ShapeDtypeStruct((sources, 1, capacity), F32),
        scratch_shapes=[pltpu.VMEM((2048, bricks * 8), BF16)],
        compiler_params=pltpu.CompilerParams(vmem_limit_bytes=VMEM_BYTES),
        name="sample_points",
    )(
        blocks,
        received,
        decoder_in,
        decoder_bias[:, None],
        decoder_out.astype(F32)[:, None],
    )[:, 0, :]


def collect_kernel(shift, width, brick_ref, slot_ref, back_ref, out_ref):
    devices, capacity = back_ref.shape
    points = brick_ref.shape[1]
    back = back_ref[...]
    high = back.astype(BF16)
    rest = back - high.astype(F32)
    mid = rest.astype(BF16)
    low = (rest - mid.astype(F32)).astype(BF16)
    pieces = jnp.concatenate([high, mid, low], axis=0)

    def block(i, carry):
        at = pl.ds(pl.multiple_of(i * width, width), width)
        owner = lax.shift_right_logical(brick_ref[:, at], shift)
        spread = (iota((capacity, width), 0) == slot_ref[:, at]).astype(F32).astype(BF16)
        found = jnp.dot(pieces, spread, preferred_element_type=F32)
        value = found[:devices] + found[devices : 2 * devices] + found[2 * devices :]
        hit = iota((devices, width), 0) == owner
        out_ref[:, at] = jnp.sum(jnp.where(hit, value, 0.0), axis=0, keepdims=True)
        return carry

    lax.fori_loop(0, points // width, block, 0)


def collect(point_brick, slot, back, bricks):
    points = point_brick.shape[0]
    return pl.pallas_call(
        functools.partial(collect_kernel, bricks.bit_length() - 1, 512),
        out_shape=jax.ShapeDtypeStruct((1, points), F32),
        compiler_params=pltpu.CompilerParams(vmem_limit_bytes=VMEM_BYTES),
        name="collect",
    )(point_brick[None, :], slot, back)[0]


def per_device(
    features,
    occupancy,
    neighbours,
    conv_weight,
    conv_bias,
    point_brick,
    point_cell,
    point_frac,
    decoder_in,
    decoder_bias,
    decoder_out,
):
    axes = ("grp", "dev")
    bricks = features.shape[0]
    devices = lax.axis_size(axes)
    me = lax.axis_index(axes)
    capacity = 2 * point_brick.shape[0] // devices
    send, slot = dispatch(point_brick, point_cell, point_frac, devices, capacity, bricks)
    received = lax.all_to_all(send, axes, split_axis=0, concat_axis=0, tiled=True)
    masked = features * occupancy[:, None, :].astype(features.dtype)
    masked = jnp.pad(masked, ((0, 1), (0, 0), (0, 0)))
    masked = jnp.transpose(masked.reshape(bricks + 1, 32, 64, 8), (0, 2, 3, 1)).reshape(
        bricks + 1, 8, 8, 256
    )
    previous = from_behind(masked[:, 7], axes, 1).astype(F32)
    following = from_behind(masked[:, 0], axes, -1).astype(F32)
    masked = masked.astype(F32)
    first = (me + jnp.repeat(jnp.arange(-1, 2, dtype=jnp.int32), 9)) * bricks
    local_nb = jnp.where(
        neighbours >= 0, jnp.clip(neighbours - first[None, :], 0, bricks - 1), bricks
    ).reshape(-1)
    blocks = conv_block(
        masked, previous, following, local_nb, occupancy, conv_weight, conv_bias
    )
    block_out = jnp.transpose(
        blocks.astype(BF16).reshape(bricks, 64, 8, 32), (0, 3, 1, 2)
    ).reshape(bricks, 32, 512)
    values = sample_points(blocks, received, decoder_in, decoder_bias, decoder_out)
    back = lax.all_to_all(values, axes, split_axis=0, concat_axis=0, tiled=True)
    return block_out, collect(point_brick, slot, back, bricks)


def solution(mesh):
    axes = ("grp", "dev")
    return jax.shard_map(
        per_device,
        mesh=mesh,
        in_specs=(
            P(axes, None, None),
            P(axes, None),
            P(axes, None),
            P(),
            P(),
            P(axes),
            P(axes),
            P(None, axes),
            P(),
            P(),
            P(),
        ),
        out_specs=(P(axes, None, None), P(axes)),
        check_vma=False,
    )
```
